32 devices in a mesh: groups: 1, node: 2 (over core), local: 16 (over z, y, x).
Axes of the slice: x: 2, y: 2, z: 4, core: 2. Of those that a mesh axis runs over, the one named last changes fastest.
Arguments:
- tokens: bfloat16 [2048, 3584], P(('groups', 'local'), 'node'), may hold values from -6 to 6
- expert_ids: int32 [2048, 8], P(('groups', 'local')), may hold values from 0 to 15, all different within a row; in each aligned block of 128 rows (0 to 127, 128 to 255, ...) at most 80 rows name the same one
- gate_probs: float32 [2048, 8], P(('groups', 'local')), may hold values from 0.05 to 1
- w_gate: bfloat16 [16, 3584, 1024], P('local', 'node'), may hold values from -0.09375 to 0.09375
- w_up: bfloat16 [16, 3584, 1024], P('local', 'node'), may hold values from -0.09375 to 0.09375
- w_down: bfloat16 [16, 1024, 3584], P('local', 'node'), may hold values from -0.1875 to 0.1875
- gate_scale: float32 [16, 1024], P('local', 'node'), may hold values from 0.5 to 2
- up_scale: float32 [16, 1024], P('local', 'node'), may hold values from 0.5 to 2
- down_scale: float32 [16, 3584], P('local'), may hold values from 0.5 to 2
- cotangent: bfloat16 [2048, 3584], P(('groups', 'local'), 'node'), may hold values from -0.19921875 to 0.19921875
Outputs:
- mixed: bfloat16 [2048, 3584], P(('groups', 'local'), 'node')
- gate_grad: float32 [2048, 8], P(('groups', 'local'))
The draws below stay inside these ranges and needn't reach their ends.
Inputs may be any that keep to these rules, and one draw needn't show every extreme that they name: `expert_ids`: each token names 8 different experts; among the tokens of one block of 128 no expert is named more than 80 times, and in every draw some expert is named exactly 80 times in some block.
All inputs are finite; a program needn't handle non-finite values.
Results may differ from the reference program's by a relative error of at most 0.018.
Values may be sent and summed in bfloat16 or wider, within the bound.
A program may use at most 128 MiB of HBM per device.

```python
import math
import jax
import jax.numpy as jnp
import numpy as np
from jax import lax

D = 3584
H = 1024
TOPK = 8
TOK_DEV = 128
EXPERTS = 16
TOKENS = 2048
CAP = 80
N_NODE = 2
N_LOCAL = 16


def level_of(own_key, dims, pieces, least, top_value):
    def one(axis_at, shards_of):
        steps = jax.random.uniform(jax.random.fold_in(jax.random.fold_in(own_key, 6), axis_at), (shards_of,), jnp.float32, least / len(pieces), top_value / len(pieces))
        return jnp.repeat(jnp.exp(steps), dims[axis_at] // shards_of).reshape((-1,) + (1,) * (len(dims) - axis_at - 1))

    factor_of = one(*pieces[0])
    for cut in pieces[1:]:
        factor_of = factor_of * one(*cut)
    return factor_of


def deal_out(key, own, number, rows, count, top, limit, lean):
    order = jax.random.permutation(key, count)
    packed, usual = shares(count, rows * top, limit, lean, True), shares(count, rows * top, limit, lean, False)
    places = jnp.arange(count)

    def named(lengths, rotation):
        used = int((lengths > 0).sum())
        fixed = max(1, used // 4)
        moved = fixed + (places - fixed + rotation * (used - fixed)) % max(1, count - fixed)
        return jnp.zeros((count,), jnp.int32).at[order[jnp.where(places < fixed, places, moved)]].set(jnp.asarray(lengths, jnp.int32))

    lengths = jnp.where(number % 4 == 0, named(packed, number // 4), named(usual, number - number // 4 - 1))
    mixed = jax.random.permutation(jax.random.fold_in(own, 3), count)
    source_of, receiver = mixed[0:count // 2 * 2:2], mixed[1:count // 2 * 2:2]
    room = jnp.minimum(lengths[source_of] - 1, limit - lengths[receiver]) // 2
    room = jnp.where((source_of == order[0]) | (receiver == order[0]) | (lengths[receiver] == 0), 0, jnp.maximum(room, 0))
    moved = jax.random.randint(jax.random.fold_in(own, 4), (count // 2,), 0, 1 << 20) % (room + 1)
    lengths = lengths.at[source_of].add(-moved).at[receiver].add(moved)
    items = jnp.searchsorted(jnp.cumsum(lengths), jnp.arange(rows * top), side="right").astype(jnp.int32)
    grid = items.reshape(top, rows).T
    grid = grid[jax.random.permutation(jax.random.fold_in(own, 1), rows)]
    rotation = jax.random.randint(jax.random.fold_in(own, 2), (rows, 1), 0, top)
    return jnp.take_along_axis(grid, (jnp.arange(top)[None, :] + rotation) % top, axis=1)


def shares(count, total, most, lean, full):
    weights = [(1 << 20) // math.isqrt(standing ** lean) + 1 for standing in range(1, count + 1)]
    largest = most if full else min(most, max(-(-total // count), total * weights[0] // sum(weights)))
    least = 1 if total - largest >= count - 1 else 0
    given, surplus = [largest] + [least] * (count - 1), total - largest - least * (count - 1)
    while surplus > 0:
        candidates = [i for i in range(1, count) if given[i] < largest] or [i for i in range(1, count) if given[i] < most]
        whole, left = sum([weights[i] for i in candidates]), surplus
        for i in candidates:
            more = min(most - given[i], max(1, left * weights[i] // whole), surplus)
            given[i] = given[i] + more
            surplus = surplus - more
    return np.array(given)


def bell_draw(key, dims, spread, bound, shards=(), kind=jnp.bfloat16):
    level = level_of(key, dims, shards, -0.22, 0.18) if shards else 1.0
    values = jax.random.normal(key, dims, jnp.float32) * spread * level
    return jnp.minimum(jnp.maximum(values, -bound), bound).astype(kind)


def setup_inputs(seed: int = 0, part: int = 0) -> dict:
    streams_of = jax.random.split(jax.random.key(seed), 11)
    part_splits = jax.random.split(jax.random.fold_in(streams_of[10], part), 11)
    tokens = bell_draw(part_splits[0], (TOKENS, D), 1.0, 6.0, ((0, 16), (1, 2)))
    expert_ids_keys = jax.random.split(jax.random.fold_in(part_splits[1], 1), TOKENS // TOK_DEV)
    expert_ids_turns = jax.random.permutation(jax.random.fold_in(part_splits[1], 3), TOKENS // TOK_DEV)
    expert_ids = jax.vmap(lambda own, number: deal_out(jax.random.fold_in(part_splits[1], 2), own, number, TOK_DEV, EXPERTS, TOPK, CAP, 1))(expert_ids_keys, expert_ids_turns).reshape((TOKENS, TOPK))
    gate_probs = jnp.clip(0.05 + 0.95 * jax.random.uniform(part_splits[2], (TOKENS, TOPK), jnp.float32) ** level_of(part_splits[2], (TOKENS, TOPK), ((0, 16),), -0.2, 0.2), 0.05, 1.0)
    w_gate = bell_draw(streams_of[3], (EXPERTS, D, H), D ** -0.5, 0.09375, ((0, 16), (1, 2)))
    w_up = bell_draw(streams_of[4], (EXPERTS, D, H), D ** -0.5, 0.09375, ((0, 16), (1, 2)))
    w_down = bell_draw(streams_of[5], (EXPERTS, H, D), H ** -0.5, 0.1875, ((0, 16), (1, 2)))
    gate_scale = jnp.clip(jnp.exp(math.log(2.0) - 1.3862944 * jax.random.uniform(streams_of[6], (EXPERTS, H), jnp.float32) ** level_of(streams_of[6], (EXPERTS, H), ((0, 16), (1, 2)), -0.2, 0.2)), 0.5, 2.0)
    up_scale = jnp.clip(jnp.exp(math.log(2.0) - 1.3862944 * jax.random.uniform(streams_of[7], (EXPERTS, H), jnp.float32) ** level_of(streams_of[7], (EXPERTS, H), ((0, 16), (1, 2)), -0.2, 0.2)), 0.5, 2.0)
    down_scale = jnp.clip(jnp.exp(math.log(2.0) - 1.3862944 * jax.random.uniform(streams_of[8], (EXPERTS, D), jnp.float32) ** level_of(streams_of[8], (EXPERTS, D), ((0, 16),), -0.2, 0.2)), 0.5, 2.0)
    cotangent = bell_draw(part_splits[9], (TOKENS, D), 0.03, 0.19921875, ((0, 16), (1, 2)))
    return dict(tokens=tokens, expert_ids=expert_ids, gate_probs=gate_probs, w_gate=w_gate, w_up=w_up, w_down=w_down, gate_scale=gate_scale, up_scale=up_scale, down_scale=down_scale, cotangent=cotangent)


def rounded(value):
    return value.astype(jnp.bfloat16).astype(jnp.float32)


def expert_rows(slot_rows, weight_gate, weight_up, weight_down, scale_gate, scale_up, scale_down):
    width = D // N_NODE
    inner = H // N_NODE
    gate_sum = jnp.zeros((slot_rows.shape[0], H), jnp.float32)
    up_sum = jnp.zeros((slot_rows.shape[0], H), jnp.float32)
    for block in range(N_NODE):
        piece = slot_rows[:, block * width:(block + 1) * width]
        gate_sum = gate_sum + rounded(jnp.dot(piece, weight_gate[block * width:(block + 1) * width], preferred_element_type=jnp.float32))
        up_sum = up_sum + rounded(jnp.dot(piece, weight_up[block * width:(block + 1) * width], preferred_element_type=jnp.float32))
    hidden = (jax.nn.silu(gate_sum * scale_gate) * (up_sum * scale_up)).astype(jnp.bfloat16)
    total = jnp.zeros((slot_rows.shape[0], D), jnp.float32)
    for block in range(N_NODE):
        term = jnp.dot(hidden[:, block * inner:(block + 1) * inner], weight_down[block * inner:(block + 1) * inner], preferred_element_type=jnp.float32)
        total = total + rounded(term * scale_down)
    return total.astype(jnp.bfloat16)


def reference(tokens, expert_ids, gate_probs, w_gate, w_up, w_down, gate_scale, up_scale, down_scale, cotangent):
    pair_count = TOK_DEV * TOPK
    blocked = expert_ids.reshape(N_LOCAL, pair_count)
    onehot = (blocked[:, :, None] == jnp.arange(EXPERTS, dtype=jnp.int32)[None, None, :]).astype(jnp.int32)
    earlier = jnp.cumsum(onehot, axis=1) - onehot
    position = jnp.sum(earlier * onehot, axis=2).astype(jnp.int32)
    source = jnp.arange(N_LOCAL, dtype=jnp.int32)[:, None]
    target = ((blocked * N_LOCAL + source) * CAP + position).reshape(-1).astype(jnp.int32)
    pair_index = jnp.arange(TOKENS * TOPK, dtype=jnp.int32)
    slot_token = jnp.full((EXPERTS * N_LOCAL * CAP,), TOKENS, jnp.int32).at[target].set(pair_index // TOPK)
    slot_pair = jnp.full((EXPERTS * N_LOCAL * CAP,), TOKENS * TOPK, jnp.int32).at[target].set(pair_index)
    padded_tokens = jnp.concatenate([tokens, jnp.zeros((1, D), tokens.dtype)], axis=0)
    padded_cot = jnp.concatenate([cotangent, jnp.zeros((1, D), cotangent.dtype)], axis=0)
    padded_probs = jnp.concatenate([gate_probs.reshape(-1), jnp.zeros((1,), jnp.float32)], axis=0)

    def visit(carry, inputs):
        combined, dots = carry
        token_index, pair_slot, weight_gate, weight_up, weight_down, scale_gate, scale_up, scale_down = inputs
        result = expert_rows(padded_tokens[token_index], weight_gate, weight_up, weight_down, scale_gate, scale_up, scale_down)
        values = result.astype(jnp.float32)
        combined = combined.at[token_index].add(padded_probs[pair_slot][:, None] * values)
        dots = dots.at[pair_slot].set(jnp.sum(values * padded_cot[token_index].astype(jnp.float32), axis=1))
        return (combined, dots), None

    start = (jnp.zeros((TOKENS + 1, D), jnp.float32), jnp.zeros((TOKENS * TOPK + 1,), jnp.float32))
    scanned = (slot_token.reshape(EXPERTS, -1), slot_pair.reshape(EXPERTS, -1), w_gate, w_up, w_down, gate_scale, up_scale, down_scale)
    (combined, dots), _ = lax.scan(visit, start, scanned)
    return combined[:TOKENS].astype(jnp.bfloat16), dots[:TOKENS * TOPK].reshape(TOKENS, TOPK)
```

```python
import jax
import jax.numpy as jnp
from jax import lax
from jax.sharding import PartitionSpec as P
from jax.experimental import pallas as pl
from jax.experimental.pallas import tpu as pltpu


MESH = pl.DeviceIdType.MESH
BF = jnp.bfloat16
F32 = jnp.float32


def on_device(
    tokens,
    expert_ids,
    gate_probs,
    w_gate,
    w_up,
    w_down,
    gate_scale,
    up_scale,
    down_scale,
    cotangent,
):
    experts = lax.axis_size("local")
    tok_rows, top_count = expert_ids.shape
    capacity = max(2, min(tok_rows, tok_rows * top_count * 5 // (4 * experts)))
    pair_count = tok_rows * top_count
    chosen = expert_ids.reshape(pair_count)
    onehot = (chosen[:, None] == jnp.arange(experts, dtype=jnp.int32)[None, :]).astype(jnp.int32)
    earlier = jnp.cumsum(onehot, axis=0) - onehot
    position = jnp.sum(earlier * onehot, axis=1)
    target = chosen * capacity + position
    owning = jnp.arange(pair_count, dtype=jnp.int32) // top_count
    features = tokens.shape[1]
    outgoing = (
        jnp.zeros((experts * capacity, features), jnp.bfloat16).at[target].set(tokens[owning])
    )
    outgoing = outgoing.reshape(experts, capacity, features)
    received = lax.all_to_all(outgoing, "local", split_axis=0, concat_axis=0, tiled=True)
    sources, slot_count, widths = received.shape
    slot_rows = received.reshape(sources * slot_count, widths)
    gate_part = jnp.dot(slot_rows, w_gate[0], preferred_element_type=jnp.float32)
    up_part = jnp.dot(slot_rows, w_up[0], preferred_element_type=jnp.float32)
    gate_sum = lax.psum_scatter(
        gate_part.astype(jnp.bfloat16), "node", scatter_dimension=1, tiled=True
    ).astype(jnp.float32)
    up_sum = lax.psum_scatter(
        up_part.astype(jnp.bfloat16), "node", scatter_dimension=1, tiled=True
    ).astype(jnp.float32)
    hidden = (jax.nn.silu(gate_sum * gate_scale[0]) * (up_sum * up_scale[0])).astype(jnp.bfloat16)
    partial_value = jnp.dot(hidden, w_down[0], preferred_element_type=jnp.float32) * down_scale[0]
    summed = lax.psum_scatter(
        partial_value.astype(jnp.bfloat16), "node", scatter_dimension=1, tiled=True
    )
    returned = lax.all_to_all(
        summed.reshape(sources, slot_count, -1), "local", split_axis=0, concat_axis=0, tiled=True
    )
    picked = returned.reshape(experts * capacity, features)[target].reshape(
        tok_rows, top_count, features
    )
    combined = jnp.sum(picked.astype(jnp.float32) * gate_probs[:, :, None], axis=1).astype(
        jnp.bfloat16
    )
    local_dots = jnp.einsum("tkf,tf->tk", picked, cotangent, preferred_element_type=jnp.float32)
    gate_grad = lax.psum(local_dots, "node")
    return (combined, gate_grad)


def layer_kernel(
    tokens, ids, probs, w_gate, w_up, w_down, gate_scale, up_scale, down_scale, cot,
    mixed, gate_grad,
    buf, w_mine, w_oth, wd, ds, codes_out, codes_in, code_mat, prob_mat,
    slots, psend, precv, mine, hid, outb, ret, acc, dots, dots_in,
    load_sem, own_sem, blk_send, blk_recv, code_send, code_recv,
    part_send, part_recv, hid_send, hid_recv, ret_send, ret_recv, wd_send, wd_recv,
    dot_send, dot_recv,
):
    experts, cap, width = outb.shape
    rows = tokens.shape[0]
    half = rows // 2
    inner = gate_scale.shape[1]
    top = ids.shape[1]
    levels = experts // 4
    me = lax.axis_index("local")
    nd = lax.axis_index("node")
    z, c = me // 4, me % 4
    y, x = c // 2, c % 2
    xn, yn = me + 1 - 2 * x, me + 2 - 4 * y
    other = 1 - nd

    def remote(src, dst, send, recv, where):
        return pltpu.make_async_remote_copy(
            src_ref=src, dst_ref=dst, send_sem=send, recv_sem=recv,
            device_id=where, device_id_type=MESH,
        )

    my_cols = pl.ds(pl.multiple_of(nd * inner, 128), inner)
    oth_cols = pl.ds(pl.multiple_of(other * inner, 128), inner)
    my_feat = pl.ds(pl.multiple_of(nd * width, 128), width)
    oth_feat = pl.ds(pl.multiple_of(other * width, 128), width)
    my_rows = pl.ds(pl.multiple_of(nd * inner, 128), inner)
    loads = [
        pltpu.make_async_copy(w_gate.at[0, :, oth_cols], w_oth.at[:, pl.ds(0, inner)], load_sem.at[0]),
        pltpu.make_async_copy(w_up.at[0, :, oth_cols], w_oth.at[:, pl.ds(inner, inner)], load_sem.at[1]),
        pltpu.make_async_copy(w_gate.at[0, :, my_cols], w_mine.at[:, pl.ds(0, inner)], load_sem.at[2]),
        pltpu.make_async_copy(w_up.at[0, :, my_cols], w_mine.at[:, pl.ds(inner, inner)], load_sem.at[3]),
        pltpu.make_async_copy(w_down.at[0, :, my_feat], wd.at[my_rows, :], load_sem.at[4]),
        pltpu.make_async_copy(down_scale.at[:, my_feat], ds, load_sem.at[5]),
    ]
    own = pltpu.make_async_copy(tokens, buf.at[me], own_sem.at[0])
    own.start()

    barrier = pltpu.get_barrier_semaphore()

    def greet(i, carry):
        pl.semaphore_signal(
            barrier, inc=1, device_id={"local": (me + i) % experts}, device_id_type=MESH
        )
        return carry

    lax.fori_loop(1, experts, greet, 0)
    pl.semaphore_signal(barrier, inc=1, device_id={"node": other}, device_id_type=MESH)
    own.wait()
    pl.semaphore_wait(barrier, experts)

    def up(b):
        return remote(buf.at[b], buf.at[b], blk_send.at[0, b], blk_recv.at[0, b], {"local": me + 4})

    def down(b):
        return remote(buf.at[b], buf.at[b], blk_send.at[1, b], blk_recv.at[0, b], {"local": me - 4})

    def to_x(b):
        return remote(buf.at[b], buf.at[b], blk_send.at[2, b], blk_recv.at[0, b], {"local": xn})

    def to_y(b):
        return remote(buf.at[b], buf.at[b], blk_send.at[3, b], blk_recv.at[0, b], {"local": yn})

    def top_x(b):
        part = buf.at[b, pl.ds(0, half), :]
        return remote(part, part, blk_send.at[4, b], blk_recv.at[1, b], {"local": xn})

    def low_y(b):
        part = buf.at[b, pl.ds(half, half), :]
        return remote(part, part, blk_send.at[5, b], blk_recv.at[2, b], {"local": yn})

    def column_step(s, act):
        if s == 0:
            act(me, z < levels - 1, z > 0)
        else:
            @pl.when(z >= s)
            def _():
                act(me - 4 * s, z < levels - 1, z < 0)

            @pl.when(z + s <= levels - 1)
            def _():
                act(me + 4 * s, z < 0, z > 0)

    def send_block(s):
        def act(b, goes_up, goes_down):
            if s > 0:
                to_x(b).wait_recv()

            @pl.when(goes_up)
            def _():
                up(b).start()

            @pl.when(goes_down)
            def _():
                down(b).start()

            to_x(b).start()
            to_y(b).start()

        column_step(s, act)

    def pass_on(s):
        def act(b, goes_up, goes_down):
            from_y = b + yn - me
            to_y(from_y).wait_recv()
            top_x(from_y).start()
            from_x = b + xn - me
            to_x(from_x).wait_recv()
            low_y(from_x).start()

        column_step(s, act)

    def sent(s):
        def act(b, goes_up, goes_down):
            @pl.when(goes_up)
            def _():
                up(b).wait_send()

            @pl.when(goes_down)
            def _():
                down(b).wait_send()

            to_x(b).wait_send()
            to_y(b).wait_send()
            top_x(b + yn - me).wait_send()
            low_y(b + xn - me).wait_send()

        column_step(s, act)

    send_block(0)
    for copy in loads:
        copy.start()
    share = remote(
        w_down.at[0, :, oth_feat], wd.at[my_rows, :], wd_send.at[0], wd_recv.at[0], {"node": other}
    )
    share.start()

    lane = lax.broadcasted_iota(jnp.int32, (rows, 128), 1)
    chosen = jnp.zeros((rows, 128), F32)
    weight = jnp.zeros((rows, 128), F32)
    for k in range(top):
        hit = ids[:, k:k + 1] == lane
        chosen = chosen + jnp.where(hit, 1.0, 0.0)
        weight = weight + jnp.where(hit, probs[:, k:k + 1], 0.0)
    before = lax.broadcasted_iota(jnp.int32, (rows, rows), 1) < lax.broadcasted_iota(
        jnp.int32, (rows, rows), 0
    )
    place = jnp.dot(
        jnp.where(before, 1.0, 0.0).astype(BF), chosen.astype(BF), preferred_element_type=F32
    )
    place = jnp.where(chosen > 0.5, place, -1.0)
    code_mat[...] = place
    prob_mat[...] = weight
    place_t = place.T
    for e in range(experts):
        codes_out[e] = jnp.broadcast_to(place_t[e:e + 1, :], (8, rows))
    codes_in[me] = codes_out[me]

    def code(to):
        return remote(
            codes_out.at[to], codes_in.at[me], code_send.at[to], code_recv.at[me], {"local": to}
        )

    def code_from(e):
        return remote(
            codes_out.at[e], codes_in.at[e], code_send.at[e], code_recv.at[e], {"local": e}
        )

    def send_code(i, carry):
        code((me + i) % experts).start()
        return carry

    lax.fori_loop(1, experts, send_code, 0)

    for s in range(1, levels):
        send_block(s)
        pass_on(s - 1)
    for copy in loads:
        copy.wait()

    def give(to):
        return remote(
            outb.at[to], ret.at[me], ret_send.at[to], ret_recv.at[me], {"local": to}
        )

    def give_from(e):
        return remote(outb.at[e], ret.at[e], ret_send.at[e], ret_recv.at[e], {"local": e})

    def column_of(g):
        gx, gy = g // 2, g % 2
        return (y + gy * (1 - 2 * y)) * 2 + x + gx * (1 - 2 * x)

    slot_row = lax.broadcasted_iota(jnp.int32, (cap, rows), 0).astype(F32)

    def run(g):
        col = column_of(g)

        def fill(i, carry):
            b = i * 4 + col

            @pl.when(b != me)
            def _():
                code_from(b).wait_recv()

            pick = jnp.where(codes_in[b][0:1, :] == slot_row, 1.0, 0.0).astype(BF)
            slots[pl.ds(pl.multiple_of(i * cap, 16), cap), :] = jnp.dot(
                pick, buf[b], preferred_element_type=F32
            ).astype(BF)
            return carry

        lax.fori_loop(0, levels, fill, 0)

        def for_other(j, carry):
            cols = pl.ds(pl.multiple_of(j * 256, 256), 256)
            psend[g, :, cols] = jnp.dot(
                slots[...], w_oth[:, cols], preferred_element_type=F32
            ).astype(BF)
            return carry

        lax.fori_loop(0, 2 * inner // 256, for_other, 0)
        part = remote(
            psend.at[g], precv.at[g], part_send.at[g], part_recv.at[g], {"node": other}
        )
        part.start()

        def for_me(j, carry):
            cols = pl.ds(pl.multiple_of(j * 256, 256), 256)
            mine[:, cols] = jnp.dot(slots[...], w_mine[:, cols], preferred_element_type=F32)
            return carry

        lax.fori_loop(0, 2 * inner // 256, for_me, 0)
        part.wait()

        def act(i, carry):
            r = pl.ds(pl.multiple_of(i * cap, 16), cap)
            gate = mine[r, 0:inner] + precv[g, r, 0:inner].astype(F32)
            upv = mine[r, inner:2 * inner] + precv[g, r, inner:2 * inner].astype(F32)
            gate = gate * gate_scale[...]
            hid[g, nd, r, :] = (gate / (1.0 + jnp.exp(-gate)) * (upv * up_scale[...])).astype(BF)
            return carry

        lax.fori_loop(0, levels, act, 0)
        swap = remote(
            hid.at[g, nd], hid.at[g, nd], hid_send.at[g], hid_recv.at[g], {"node": other}
        )
        swap.start()
        swap.wait()

        def project(j, carry):
            cols = pl.ds(pl.multiple_of(j * 256, 256), 256)
            value = jnp.dot(hid[g, 0], wd[0:inner, cols], preferred_element_type=F32)
            value = value + jnp.dot(
                hid[g, 1], wd[inner:2 * inner, cols], preferred_element_type=F32
            )
            value = (value * ds[:, cols]).astype(BF)
            for i in range(levels):
                outb[i * 4 + col, :, cols] = value[i * cap:(i + 1) * cap]
            return carry

        lax.fori_loop(0, width // 256, project, 0)

        def back(i, carry):
            b = i * 4 + col

            @pl.when(b != me)
            def _():
                give(b).start()

            return carry

        lax.fori_loop(0, levels, back, 0)

    share.wait()
    run(0)
    keep = pltpu.make_async_copy(outb.at[me], ret.at[me], own_sem.at[1])
    keep.start()
    pass_on(levels - 1)

    def later(g, carry):
        @pl.when(g == 3)
        def _():
            def diag(i, inner_carry):
                b = i * 4 + 3 - c
                top_x(b).wait_recv()
                low_y(b).wait_recv()
                return inner_carry

            lax.fori_loop(0, levels, diag, 0)

        run(g)
        return carry

    lax.fori_loop(1, 4, later, 0)
    keep.wait()

    acc[...] = jnp.zeros_like(acc)
    dots[...] = jnp.zeros_like(dots)
    slot_lane = lax.broadcasted_iota(jnp.int32, (rows, cap), 1).astype(F32)

    def combine(i, carry):
        e = (i % levels) * 4 + column_of(i // levels)

        @pl.when(e != me)
        def _():
            give_from(e).wait_recv()

        at_e = lane == e
        slot = jnp.sum(jnp.where(at_e, code_mat[...], 0.0), axis=1, keepdims=True)
        prob = jnp.sum(jnp.where(at_e, prob_mat[...], 0.0), axis=1, keepdims=True)
        pick = jnp.where(slot == slot_lane, 1.0, 0.0).astype(BF)
        total = jnp.zeros((rows, 1), F32)
        for j in range(width // 256):
            cols = slice(j * 256, (j + 1) * 256)
            got = jnp.dot(pick, ret[e, :, cols], preferred_element_type=F32)
            acc[:, cols] += got * prob
            total = total + jnp.sum(got * cot[:, cols].astype(F32), axis=1, keepdims=True)
        dots[...] = jnp.where(at_e, total, dots[...])
        return carry

    lax.fori_loop(0, experts, combine, 0)
    join = remote(dots, dots_in, dot_send.at[0], dot_recv.at[0], {"node": other})
    join.start()
    mixed[...] = acc[...].astype(BF)
    join.wait()
    both = dots[...] + dots_in[...]
    small = lax.broadcasted_iota(jnp.int32, (rows, top), 1)
    grads = jnp.zeros((rows, top), F32)
    for k in range(top):
        one = jnp.sum(jnp.where(ids[:, k:k + 1] == lane, both, 0.0), axis=1, keepdims=True)
        grads = jnp.where(small == k, one, grads)
    gate_grad[...] = grads

    for s in range(levels):
        sent(s)

    def finish(i, carry):
        to = (me + i) % experts
        code(to).wait_send()
        give(to).wait_send()
        return carry

    lax.fori_loop(1, experts, finish, 0)


def fused(
    tokens, expert_ids, gate_probs, w_gate, w_up, w_down, gate_scale, up_scale, down_scale, cotangent
):
    experts = lax.axis_size("local")
    rows, top = expert_ids.shape
    cap = max(2, min(rows, rows * top * 5 // (4 * experts)))
    width = tokens.shape[1]
    inner = w_down.shape[1]
    levels = experts // 4
    m = levels * cap
    vm = pl.BlockSpec(memory_space=pltpu.VMEM)
    hbm = pl.BlockSpec(memory_space=pl.ANY)
    dma = pltpu.SemaphoreType.DMA
    return pl.pallas_call(
        layer_kernel,
        out_shape=(
            jax.ShapeDtypeStruct((rows, width), BF),
            jax.ShapeDtypeStruct((rows, top), F32),
        ),
        in_specs=[hbm, vm, vm, hbm, hbm, hbm, vm, vm, hbm, vm],
        out_specs=(vm, vm),
        scratch_shapes=[
            pltpu.VMEM((experts, rows, width), BF),
            pltpu.VMEM((width, 2 * inner), BF),
            pltpu.VMEM((width, 2 * inner), BF),
            pltpu.VMEM((2 * inner, width), BF),
            pltpu.VMEM((1, width), F32),
            pltpu.VMEM((experts, 8, rows), F32),
            pltpu.VMEM((experts, 8, rows), F32),
            pltpu.VMEM((rows, 128), F32),
            pltpu.VMEM((rows, 128), F32),
            pltpu.VMEM((m, width), BF),
            pltpu.VMEM((4, m, 2 * inner), BF),
            pltpu.VMEM((4, m, 2 * inner), BF),
            pltpu.VMEM((m, 2 * inner), F32),
            pltpu.VMEM((4, 2, m, inner), BF),
            pltpu.VMEM((experts, cap, width), BF),
            pltpu.VMEM((experts, cap, width), BF),
            pltpu.VMEM((rows, width), F32),
            pltpu.VMEM((rows, 128), F32),
            pltpu.VMEM((rows, 128), F32),
            dma((6,)),
            dma((2,)),
            dma((6, experts)),
            dma((3, experts)),
            dma((experts,)),
            dma((experts,)),
            dma((4,)),
            dma((4,)),
            dma((4,)),
            dma((4,)),
            dma((experts,)),
            dma((experts,)),
            dma((1,)),
            dma((1,)),
            dma((1,)),
            dma((1,)),
        ],
        compiler_params=pltpu.CompilerParams(
            collective_id=0, has_side_effects=True, vmem_limit_bytes=56 * 1024 * 1024
        ),
    )(
        tokens, expert_ids, gate_probs, w_gate, w_up, w_down, gate_scale, up_scale, down_scale,
        cotangent,
    )


def solution(mesh):
    small = mesh.shape["local"] == 16 and mesh.shape["node"] == 2
    return jax.shard_map(
        fused if small else on_device,
        mesh=mesh,
        in_specs=(
            P(("groups", "local"), "node"),
            P(("groups", "local"), None),
            P(("groups", "local"), None),
            P("local", "node", None),
            P("local", "node", None),
            P("local", "node", None),
            P("local", "node"),
            P("local", "node"),
            P("local", None),
            P(("groups", "local"), "node"),
        ),
        out_specs=(P(("groups", "local"), "node"), P(("groups", "local"), None)),
        check_vma=False,
    )
```

```python
import jax
import jax.numpy as jnp
from jax import lax
from jax.sharding import PartitionSpec as P
from jax.experimental import pallas as pl
from jax.experimental.pallas import tpu as pltpu


MESH = pl.DeviceIdType.MESH
BF = jnp.bfloat16
F32 = jnp.float32


def on_device(
    tokens,
    expert_ids,
    gate_probs,
    w_gate,
    w_up,
    w_down,
    gate_scale,
    up_scale,
    down_scale,
    cotangent,
):
    experts = lax.axis_size("local")
    tok_rows, top_count = expert_ids.shape
    capacity = max(2, min(tok_rows, tok_rows * top_count * 5 // (4 * experts)))
    pair_count = tok_rows * top_count
    chosen = expert_ids.reshape(pair_count)
    onehot = (chosen[:, None] == jnp.arange(experts, dtype=jnp.int32)[None, :]).astype(jnp.int32)
    earlier = jnp.cumsum(onehot, axis=0) - onehot
    position = jnp.sum(earlier * onehot, axis=1)
    target = chosen * capacity + position
    owning = jnp.arange(pair_count, dtype=jnp.int32) // top_count
    features = tokens.shape[1]
    outgoing = (
        jnp.zeros((experts * capacity, features), jnp.bfloat16).at[target].set(tokens[owning])
    )
    outgoing = outgoing.reshape(experts, capacity, features)
    received = lax.all_to_all(outgoing, "local", split_axis=0, concat_axis=0, tiled=True)
    sources, slot_count, widths = received.shape
    slot_rows = received.reshape(sources * slot_count, widths)
    gate_part = jnp.dot(slot_rows, w_gate[0], preferred_element_type=jnp.float32)
    up_part = jnp.dot(slot_rows, w_up[0], preferred_element_type=jnp.float32)
    gate_sum = lax.psum_scatter(
        gate_part.astype(jnp.bfloat16), "node", scatter_dimension=1, tiled=True
    ).astype(jnp.float32)
    up_sum = lax.psum_scatter(
        up_part.astype(jnp.bfloat16), "node", scatter_dimension=1, tiled=True
    ).astype(jnp.float32)
    hidden = (jax.nn.silu(gate_sum * gate_scale[0]) * (up_sum * up_scale[0])).astype(jnp.bfloat16)
    partial_value = jnp.dot(hidden, w_down[0], preferred_element_type=jnp.float32) * down_scale[0]
    summed = lax.psum_scatter(
        partial_value.astype(jnp.bfloat16), "node", scatter_dimension=1, tiled=True
    )
    returned = lax.all_to_all(
        summed.reshape(sources, slot_count, -1), "local", split_axis=0, concat_axis=0, tiled=True
    )
    picked = returned.reshape(experts * capacity, features)[target].reshape(
        tok_rows, top_count, features
    )
    combined = jnp.sum(picked.astype(jnp.float32) * gate_probs[:, :, None], axis=1).astype(
        jnp.bfloat16
    )
    local_dots = jnp.einsum("tkf,tf->tk", picked, cotangent, preferred_element_type=jnp.float32)
    gate_grad = lax.psum(local_dots, "node")
    return (combined, gate_grad)


def layer_kernel(
    tokens, ids, probs, w_gate, w_up, w_down, gate_scale, up_scale, down_scale, cot,
    mixed, gate_grad,
    blk, cotb, info, w_mine, w_oth, wd, ds, picked, slots, psend, precv, mine, hid,
    outb, ret, acc, part_out, part_in, dots_out, dots_in, dots, dots_core,
    load_sem, own_sem, keep_sem, line_send, line_recv, disp_send, disp_recv,
    gu_send, gu_recv, hid_send, hid_recv, ret_send, ret_recv, back_send, back_recv,
    core_send, core_recv,
):
    levels, rows, width = blk.shape
    plane, cap = ret.shape[1], ret.shape[2]
    inner = gate_scale.shape[1]
    top = ids.shape[1]
    experts = levels * plane
    me = lax.axis_index("local")
    nd = lax.axis_index("node")
    z, c = me // 4, me % 4
    y, x = c // 2, c % 2
    other = 1 - nd

    def remote(src, dst, send, recv, where):
        return pltpu.make_async_remote_copy(
            src_ref=src, dst_ref=dst, send_sem=send, recv_sem=recv,
            device_id=where, device_id_type=MESH,
        )

    order = [z, 1 + z % 2, 3 - 3 * (z // 2), 2 - 2 * (z % 2) + z // 2]

    def column(j):
        return (y + (j // 2) * (1 - 2 * y)) * 2 + x + (j % 2) * (1 - 2 * x)

    my_cols = pl.ds(pl.multiple_of(nd * inner, 128), inner)
    oth_cols = pl.ds(pl.multiple_of(other * inner, 128), inner)
    my_feat = pl.ds(pl.multiple_of(nd * width, 128), width)
    oth_feat = pl.ds(pl.multiple_of(other * width, 128), width)
    my_rows = pl.ds(pl.multiple_of(nd * inner, 128), inner)
    loads = [
        pltpu.make_async_copy(w_gate.at[0, :, oth_cols], w_oth.at[:, pl.ds(0, inner)], load_sem.at[0]),
        pltpu.make_async_copy(w_up.at[0, :, oth_cols], w_oth.at[:, pl.ds(inner, inner)], load_sem.at[1]),
        pltpu.make_async_copy(w_gate.at[0, :, my_cols], w_mine.at[:, pl.ds(0, inner)], load_sem.at[2]),
        pltpu.make_async_copy(w_up.at[0, :, my_cols], w_mine.at[:, pl.ds(inner, inner)], load_sem.at[3]),
        pltpu.make_async_copy(w_down.at[0, :, my_feat], wd.at[my_rows, :], load_sem.at[4]),
        pltpu.make_async_copy(down_scale.at[:, my_feat], ds, load_sem.at[5]),
    ]
    own = [
        pltpu.make_async_copy(tokens, blk.at[z], own_sem.at[0]),
        pltpu.make_async_copy(cot, cotb.at[z], own_sem.at[1]),
    ]
    for copy in own:
        copy.start()

    barrier = pltpu.get_barrier_semaphore()
    for i in range(1, levels):
        pl.semaphore_signal(
            barrier, inc=1, device_id={"local": (me + plane * i) % experts}, device_id_type=MESH
        )
    for j in range(1, plane):
        pl.semaphore_signal(
            barrier, inc=1, device_id={"local": z * plane + column(j)}, device_id_type=MESH
        )
    pl.semaphore_signal(barrier, inc=1, device_id={"node": other}, device_id_type=MESH)

    lane = lax.broadcasted_iota(jnp.int32, (rows, 128), 1)
    chosen = jnp.zeros((rows, 128), F32)
    weight = jnp.zeros((rows, 128), F32)
    for k in range(top):
        hit = ids[:, k:k + 1] == lane
        chosen = chosen + jnp.where(hit, 1.0, 0.0)
        weight = weight + jnp.where(hit, probs[:, k:k + 1], 0.0)
    before = lax.broadcasted_iota(jnp.int32, (rows, rows), 1) < lax.broadcasted_iota(
        jnp.int32, (rows, rows), 0
    )
    place = jnp.dot(
        jnp.where(before, 1.0, 0.0).astype(BF), chosen.astype(BF), preferred_element_type=F32
    )
    place = jnp.where(chosen > 0.5, place, -1.0)
    info[z, 0:rows, :] = place
    info[z, rows:2 * rows, :] = weight
    info[z, 2 * rows:2 * rows + experts, :] = place.T[0:experts, :]
    for copy in own:
        copy.wait()
    pl.semaphore_wait(barrier, levels + plane - 1)

    items = (info, blk, cotb)

    def line(item, up, b):
        return remote(
            items[item].at[b], items[item].at[b],
            line_send.at[1 - up, item, b], line_recv.at[item, b],
            {"local": me - plane + 2 * plane * up},
        )

    def line_step(s, act):
        if s == 0:
            act(z, z < levels - 1, z > 0)
        else:
            @pl.when(z >= s)
            def _():
                act(z - s, z < levels - 1, z < 0)

            @pl.when(z + s <= levels - 1)
            def _():
                act(z + s, z < 0, z > 0)

    def spread(s, which):
        def act(b, goes_up, goes_down):
            for item in which:
                if s > 0:
                    line(item, 1, b).wait_recv()

                @pl.when(goes_up)
                def _():
                    line(item, 1, b).start()

                @pl.when(goes_down)
                def _():
                    line(item, 0, b).start()

        line_step(s, act)

    def spread_done(s):
        def act(b, goes_up, goes_down):
            for item in range(3):
                @pl.when(goes_up)
                def _():
                    line(item, 1, b).wait_send()

                @pl.when(goes_down)
                def _():
                    line(item, 0, b).wait_send()

        line_step(s, act)

    slot_row = lax.broadcasted_iota(jnp.int32, (cap, rows), 0).astype(F32)

    def slots_of(i):
        return pl.ds(pl.multiple_of(i * cap, 16), cap)

    def disp(b, to):
        return remote(
            picked.at[b, to], slots.at[b, slots_of(c), :],
            disp_send.at[b, to], disp_recv.at[b, c], {"local": z * plane + to},
        )

    def disp_from(b, i):
        return remote(
            picked.at[b, i], slots.at[b, slots_of(i), :],
            disp_send.at[b, i], disp_recv.at[b, i], {"local": z * plane + i},
        )

    def dispatch(b):
        for j in (3, 1, 2, 0):
            to = column(j)
            code = info[b, pl.ds(2 * rows + z * plane + to, 1), :]
            pick = jnp.where(code == slot_row, 1.0, 0.0).astype(BF)
            for n in range(width // 256):
                cols = slice(n * 256, (n + 1) * 256)
                value = jnp.dot(pick, blk[b, :, cols], preferred_element_type=F32).astype(BF)
                if j == 0:
                    slots[b, slots_of(c), cols] = value
                else:
                    picked[b, to, :, cols] = value
            if j > 0:
                disp(b, to).start()

    def give(b, to):
        return remote(
            outb.at[b, slots_of(to), :], ret.at[b, c],
            ret_send.at[b, to], ret_recv.at[b, c], {"local": z * plane + to},
        )

    def give_from(b, i):
        return remote(
            outb.at[b, slots_of(i), :], ret.at[b, i],
            ret_send.at[b, i], ret_recv.at[b, i], {"local": z * plane + i},
        )

    def keep(b):
        return pltpu.make_async_copy(outb.at[b, slots_of(c), :], ret.at[b, c], keep_sem.at[b])

    def run(b):
        for j in range(1, plane):
            disp_from(b, column(j)).wait_recv()

        def for_other(n, carry):
            cols = pl.ds(pl.multiple_of(n * 256, 256), 256)
            psend[b, :, cols] = jnp.dot(
                slots[b], w_oth[:, cols], preferred_element_type=F32
            ).astype(BF)
            return carry

        lax.fori_loop(0, 2 * inner // 256, for_other, 0)
        part = remote(psend.at[b], precv.at[b], gu_send.at[b], gu_recv.at[b], {"node": other})
        part.start()

        def for_me(n, carry):
            cols = pl.ds(pl.multiple_of(n * 256, 256), 256)
            mine[:, cols] = jnp.dot(slots[b], w_mine[:, cols], preferred_element_type=F32)
            return carry

        lax.fori_loop(0, 2 * inner // 256, for_me, 0)
        part.wait()

        def act(i, carry):
            r = slots_of(i)
            gate = mine[r, 0:inner] + precv[b, r, 0:inner].astype(F32)
            upv = mine[r, inner:2 * inner] + precv[b, r, inner:2 * inner].astype(F32)
            gate = gate * gate_scale[...]
            hid[b, nd, r, :] = (gate / (1.0 + jnp.exp(-gate)) * (upv * up_scale[...])).astype(BF)
            return carry

        lax.fori_loop(0, plane, act, 0)
        swap = remote(
            hid.at[b, nd], hid.at[b, nd], hid_send.at[b], hid_recv.at[b], {"node": other}
        )
        swap.start()
        swap.wait()

        def project(n, carry):
            cols = pl.ds(pl.multiple_of(n * 256, 256), 256)
            value = jnp.dot(hid[b, 0], wd[0:inner, cols], preferred_element_type=F32)
            value = value + jnp.dot(
                hid[b, 1], wd[inner:2 * inner, cols], preferred_element_type=F32
            )
            outb[b, :, cols] = (value * ds[:, cols]).astype(BF)
            return carry

        lax.fori_loop(0, width // 256, project, 0)
        for j in (3, 1, 2):
            give(b, column(j)).start()
        keep(b).start()

    slot_lane = lax.broadcasted_iota(jnp.int32, (rows, cap), 1).astype(F32)

    def home(b):
        to = {"local": b * plane + c}
        return (
            remote(part_out.at[b], part_in.at[z], back_send.at[0, b], back_recv.at[0, z], to),
            remote(dots_out.at[b], dots_in.at[z], back_send.at[1, b], back_recv.at[1, z], to),
        )

    def home_from(b):
        to = {"local": b * plane + c}
        return (
            remote(part_out.at[b], part_in.at[b], back_send.at[0, b], back_recv.at[0, b], to),
            remote(dots_out.at[b], dots_in.at[b], back_send.at[1, b], back_recv.at[1, b], to),
        )

    def combine(b, stays):
        acc[...] = jnp.zeros_like(acc)
        dots[...] = jnp.zeros_like(dots)

        def one(j, carry):
            i = column(j)

            @pl.when(j > 0)
            def _():
                give_from(b, i).wait_recv()

            at_e = lane == z * plane + i
            slot = jnp.sum(jnp.where(at_e, info[b, 0:rows, :], 0.0), axis=1, keepdims=True)
            prob = jnp.sum(
                jnp.where(at_e, info[b, rows:2 * rows, :], 0.0), axis=1, keepdims=True
            )
            pick = jnp.where(slot == slot_lane, 1.0, 0.0).astype(BF)
            total = jnp.zeros((rows, 1), F32)
            for n in range(width // 256):
                cols = slice(n * 256, (n + 1) * 256)
                got = jnp.dot(pick, ret[b, i, :, cols], preferred_element_type=F32)
                acc[:, cols] += got * prob
                total = total + jnp.sum(
                    got * cotb[b, :, cols].astype(F32), axis=1, keepdims=True
                )
            dots[...] = jnp.where(at_e, total, dots[...])
            return carry

        keep(b).wait()
        lax.fori_loop(0, plane, one, 0)
        if stays:
            part_in[b] = acc[...].astype(BF)
            dots_in[b] = dots[...]
        else:
            part_out[b] = acc[...].astype(BF)
            dots_out[b] = dots[...]
            for copy in home(b):
                copy.start()

    spread(0, (0, 1))
    for copy in loads:
        copy.start()
    share = remote(
        w_down.at[0, :, oth_feat], wd.at[my_rows, :], core_send.at[0], core_recv.at[0],
        {"node": other},
    )
    share.start()
    dispatch(order[0])
    spread(1, (0, 1))
    dispatch(order[1])
    spread(2, (0, 1))
    for copy in loads:
        copy.wait()
    share.wait()
    run(order[0])
    spread(3, (0, 1))
    spread(0, (2,))
    dispatch(order[2])
    dispatch(order[3])
    run(order[1])
    spread(1, (2,))
    combine(order[0], True)
    spread(2, (2,))
    run(order[2])
    spread(3, (2,))
    combine(order[1], False)
    run(order[3])
    combine(order[2], False)
    combine(order[3], False)

    for s in range(1, levels):
        for copy in home_from((z + s) % levels):
            copy.wait_recv()
    dots[...] = dots_in[0] + dots_in[1] + dots_in[2] + dots_in[3]
    join = remote(dots, dots_core, core_send.at[1], core_recv.at[1], {"node": other})
    join.start()
    for n in range(width // 256):
        cols = slice(n * 256, (n + 1) * 256)
        total = part_in[0, :, cols].astype(F32)
        for i in range(1, levels):
            total = total + part_in[i, :, cols].astype(F32)
        mixed[:, cols] = total.astype(BF)
    join.wait()
    both = dots[...] + dots_core[...]
    small = lax.broadcasted_iota(jnp.int32, (rows, top), 1)
    grads = jnp.zeros((rows, top), F32)
    for k in range(top):
        one = jnp.sum(jnp.where(ids[:, k:k + 1] == lane, both, 0.0), axis=1, keepdims=True)
        grads = jnp.where(small == k, one, grads)
    gate_grad[...] = grads

    for s in range(levels):
        spread_done(s)
    for i in range(levels):
        for j in range(1, plane):
            disp(i, column(j)).wait_send()
            give(i, column(j)).wait_send()
    for s in range(1, levels):
        for copy in home((z + s) % levels):
            copy.wait_send()


def fused(
    tokens, expert_ids, gate_probs, w_gate, w_up, w_down, gate_scale, up_scale, down_scale, cotangent
):
    experts = lax.axis_size("local")
    rows, top = expert_ids.shape
    cap = max(2, min(rows, rows * top * 5 // (4 * experts)))
    width = tokens.shape[1]
    inner = w_down.shape[1]
    plane = 4
    levels = experts // plane
    m = plane * cap
    vm = pl.BlockSpec(memory_space=pltpu.VMEM)
    hbm = pl.BlockSpec(memory_space=pl.ANY)
    dma = pltpu.SemaphoreType.DMA
    return pl.pallas_call(
        layer_kernel,
        out_shape=(
            jax.ShapeDtypeStruct((rows, width), BF),
            jax.ShapeDtypeStruct((rows, top), F32),
        ),
        in_specs=[hbm, vm, vm, hbm, hbm, hbm, vm, vm, hbm, hbm],
        out_specs=(vm, vm),
        scratch_shapes=[
            pltpu.VMEM((levels, rows, width), BF),
            pltpu.VMEM((levels, rows, width), BF),
            pltpu.VMEM((levels, 2 * rows + experts, 128), F32),
            pltpu.VMEM((width, 2 * inner), BF),
            pltpu.VMEM((width, 2 * inner), BF),
            pltpu.VMEM((2 * inner, width), BF),
            pltpu.VMEM((1, width), F32),
            pltpu.VMEM((levels, plane, cap, width), BF),
            pltpu.VMEM((levels, m, width), BF),
            pltpu.VMEM((levels, m, 2 * inner), BF),
            pltpu.VMEM((levels, m, 2 * inner), BF),
            pltpu.VMEM((m, 2 * inner), F32),
            pltpu.VMEM((levels, 2, m, inner), BF),
            pltpu.VMEM((levels, m, width), BF),
            pltpu.VMEM((levels, plane, cap, width), BF),
            pltpu.VMEM((rows, width), F32),
            pltpu.VMEM((levels, rows, width), BF),
            pltpu.VMEM((levels, rows, width), BF),
            pltpu.VMEM((levels, rows, 128), F32),
            pltpu.VMEM((levels, rows, 128), F32),
            pltpu.VMEM((rows, 128), F32),
            pltpu.VMEM((rows, 128), F32),
            dma((6,)),
            dma((2,)),
            dma((levels,)),
            dma((2, 3, levels)),
            dma((3, levels)),
            dma((levels, plane)),
            dma((levels, plane)),
            dma((levels,)),
            dma((levels,)),
            dma((levels,)),
            dma((levels,)),
            dma((levels, plane)),
            dma((levels, plane)),
            dma((2, levels)),
            dma((2, levels)),
            dma((2,)),
            dma((2,)),
        ],
        compiler_params=pltpu.CompilerParams(
            collective_id=0, has_side_effects=True, vmem_limit_bytes=58 * 1024 * 1024
        ),
    )(
        tokens, expert_ids, gate_probs, w_gate, w_up, w_down, gate_scale, up_scale, down_scale,
        cotangent,
    )


def solution(mesh):
    small = mesh.shape["local"] == 16 and mesh.shape["node"] == 2
    return jax.shard_map(
        fused if small else on_device,
        mesh=mesh,
        in_specs=(
            P(("groups", "local"), "node"),
            P(("groups", "local"), None),
            P(("groups", "local"), None),
            P("local", "node", None),
            P("local", "node", None),
            P("local", "node", None),
            P("local", "node"),
            P("local", "node"),
            P("local", None),
            P(("groups", "local"), "node"),
        ),
        out_specs=(P(("groups", "local"), "node"), P(("groups", "local"), None)),
        check_vma=False,
    )
```

```python
import jax
import jax.numpy as jnp
from jax import lax
from jax.sharding import PartitionSpec as P
from jax.experimental import pallas as pl
from jax.experimental.pallas import tpu as pltpu


MESH = pl.DeviceIdType.MESH
BF = jnp.bfloat16
F32 = jnp.float32


def on_device(
    tokens,
    expert_ids,
    gate_probs,
    w_gate,
    w_up,
    w_down,
    gate_scale,
    up_scale,
    down_scale,
    cotangent,
):
    experts = lax.axis_size("local")
    tok_rows, top_count = expert_ids.shape
    capacity = max(2, min(tok_rows, tok_rows * top_count * 5 // (4 * experts)))
    pair_count = tok_rows * top_count
    chosen = expert_ids.reshape(pair_count)
    onehot = (chosen[:, None] == jnp.arange(experts, dtype=jnp.int32)[None, :]).astype(jnp.int32)
    earlier = jnp.cumsum(onehot, axis=0) - onehot
    position = jnp.sum(earlier * onehot, axis=1)
    target = chosen * capacity + position
    owning = jnp.arange(pair_count, dtype=jnp.int32) // top_count
    features = tokens.shape[1]
    outgoing = (
        jnp.zeros((experts * capacity, features), jnp.bfloat16).at[target].set(tokens[owning])
    )
    outgoing = outgoing.reshape(experts, capacity, features)
    received = lax.all_to_all(outgoing, "local", split_axis=0, concat_axis=0, tiled=True)
    sources, slot_count, widths = received.shape
    slot_rows = received.reshape(sources * slot_count, widths)
    gate_part = jnp.dot(slot_rows, w_gate[0], preferred_element_type=jnp.float32)
    up_part = jnp.dot(slot_rows, w_up[0], preferred_element_type=jnp.float32)
    gate_sum = lax.psum_scatter(
        gate_part.astype(jnp.bfloat16), "node", scatter_dimension=1, tiled=True
    ).astype(jnp.float32)
    up_sum = lax.psum_scatter(
        up_part.astype(jnp.bfloat16), "node", scatter_dimension=1, tiled=True
    ).astype(jnp.float32)
    hidden = (jax.nn.silu(gate_sum * gate_scale[0]) * (up_sum * up_scale[0])).astype(jnp.bfloat16)
    partial_value = jnp.dot(hidden, w_down[0], preferred_element_type=jnp.float32) * down_scale[0]
    summed = lax.psum_scatter(
        partial_value.astype(jnp.bfloat16), "node", scatter_dimension=1, tiled=True
    )
    returned = lax.all_to_all(
        summed.reshape(sources, slot_count, -1), "local", split_axis=0, concat_axis=0, tiled=True
    )
    picked = returned.reshape(experts * capacity, features)[target].reshape(
        tok_rows, top_count, features
    )
    combined = jnp.sum(picked.astype(jnp.float32) * gate_probs[:, :, None], axis=1).astype(
        jnp.bfloat16
    )
    local_dots = jnp.einsum("tkf,tf->tk", picked, cotangent, preferred_element_type=jnp.float32)
    gate_grad = lax.psum(local_dots, "node")
    return (combined, gate_grad)


def layer_kernel(
    tokens, ids, probs, w_gate, w_up, w_down, gate_scale, up_scale, down_scale, cot,
    mixed, gate_grad,
    blk, cotb, info, w_mine, w_oth, wd, ds, picked, slots, psend, precv, mine, hid,
    outb, ret, acc, part_out, part_in, dots_out, dots_in, table, dots, dots_sum, dots_core,
    load_sem, own_sem, keep_sem, line_send, line_recv, disp_send, disp_recv,
    gu_send, gu_recv, hid_send, hid_recv, ret_send, ret_recv, back_send, back_recv,
    core_send, core_recv,
):
    levels, rows, width = blk.shape
    plane, cap = ret.shape[1], ret.shape[2]
    inner = gate_scale.shape[1]
    top = ids.shape[0]
    experts = levels * plane
    me = lax.axis_index("local")
    nd = lax.axis_index("node")
    z, c = me // 4, me % 4
    y, x = c // 2, c % 2
    other = 1 - nd

    def remote(src, dst, send, recv, where):
        return pltpu.make_async_remote_copy(
            src_ref=src, dst_ref=dst, send_sem=send, recv_sem=recv,
            device_id=where, device_id_type=MESH,
        )

    order = [z, 1 + z % 2, 3 - 3 * (z // 2), 2 - 2 * (z % 2) + z // 2]

    def column(j):
        return (y + (j // 2) * (1 - 2 * y)) * 2 + x + (j % 2) * (1 - 2 * x)

    my_cols = pl.ds(pl.multiple_of(nd * inner, 128), inner)
    oth_cols = pl.ds(pl.multiple_of(other * inner, 128), inner)
    my_feat = pl.ds(pl.multiple_of(nd * width, 128), width)
    oth_feat = pl.ds(pl.multiple_of(other * width, 128), width)
    my_rows = pl.ds(pl.multiple_of(nd * inner, 128), inner)
    loads = [
        pltpu.make_async_copy(w_gate.at[0, :, oth_cols], w_oth.at[:, pl.ds(0, inner)], load_sem.at[0]),
        pltpu.make_async_copy(w_up.at[0, :, oth_cols], w_oth.at[:, pl.ds(inner, inner)], load_sem.at[1]),
        pltpu.make_async_copy(w_gate.at[0, :, my_cols], w_mine.at[:, pl.ds(0, inner)], load_sem.at[2]),
        pltpu.make_async_copy(w_up.at[0, :, my_cols], w_mine.at[:, pl.ds(inner, inner)], load_sem.at[3]),
        pltpu.make_async_copy(w_down.at[0, :, my_feat], wd.at[my_rows, :], load_sem.at[4]),
        pltpu.make_async_copy(down_scale.at[:, my_feat], ds, load_sem.at[5]),
    ]
    own = [
        pltpu.make_async_copy(tokens, blk.at[z], own_sem.at[0]),
        pltpu.make_async_copy(cot, cotb.at[z], own_sem.at[1]),
    ]
    for copy in own:
        copy.start()

    barrier = pltpu.get_barrier_semaphore()
    for i in range(1, levels):
        pl.semaphore_signal(
            barrier, inc=1, device_id={"local": (me + plane * i) % experts}, device_id_type=MESH
        )
    for j in range(1, plane):
        pl.semaphore_signal(
            barrier, inc=1, device_id={"local": z * plane + column(j)}, device_id_type=MESH
        )
    pl.semaphore_signal(barrier, inc=1, device_id={"node": other}, device_id_type=MESH)

    expert_row = lax.broadcasted_iota(jnp.int32, (experts, rows), 0)
    chosen = jnp.zeros((experts, rows), F32)
    weight = jnp.zeros((experts, rows), F32)
    for k in range(top):
        hit = ids[k:k + 1, :] == expert_row
        chosen = chosen + jnp.where(hit, 1.0, 0.0)
        weight = weight + jnp.where(hit, probs[k:k + 1, :], 0.0)
    before = lax.broadcasted_iota(jnp.int32, (rows, rows), 0) < lax.broadcasted_iota(
        jnp.int32, (rows, rows), 1
    )
    place = jnp.dot(
        chosen.astype(BF), jnp.where(before, 1.0, 0.0).astype(BF), preferred_element_type=F32
    )
    info[z, 0:experts, :] = jnp.where(chosen > 0.5, place, -1.0)
    info[z, experts:2 * experts, :] = weight
    for copy in own:
        copy.wait()
    pl.semaphore_wait(barrier, levels + plane - 1)

    items = (info, blk, cotb)

    def line(item, up, b):
        return remote(
            items[item].at[b], items[item].at[b],
            line_send.at[1 - up, item, b], line_recv.at[item, b],
            {"local": me - plane + 2 * plane * up},
        )

    def line_step(s, act):
        if s == 0:
            act(z, z < levels - 1, z > 0)
        else:
            @pl.when(z >= s)
            def _():
                act(z - s, z < levels - 1, z < 0)

            @pl.when(z + s <= levels - 1)
            def _():
                act(z + s, z < 0, z > 0)

    def spread(s, which):
        def act(b, goes_up, goes_down):
            for item in which:
                if s > 0:
                    line(item, 1, b).wait_recv()

                @pl.when(goes_up)
                def _():
                    line(item, 1, b).start()

                @pl.when(goes_down)
                def _():
                    line(item, 0, b).start()

        line_step(s, act)

    def spread_done(s):
        def act(b, goes_up, goes_down):
            for item in range(3):
                @pl.when(goes_up)
                def _():
                    line(item, 1, b).wait_send()

                @pl.when(goes_down)
                def _():
                    line(item, 0, b).wait_send()

        line_step(s, act)

    slot_row = lax.broadcasted_iota(jnp.int32, (cap, rows), 0).astype(F32)

    def slots_of(i):
        return pl.ds(pl.multiple_of(i * cap, 16), cap)

    def disp(b, to):
        return remote(
            picked.at[b, to], slots.at[b, slots_of(c), :],
            disp_send.at[b, to], disp_recv.at[b, c], {"local": z * plane + to},
        )

    def disp_from(b, i):
        return remote(
            picked.at[b, i], slots.at[b, slots_of(i), :],
            disp_send.at[b, i], disp_recv.at[b, i], {"local": z * plane + i},
        )

    def dispatch(b):
        for j in (3, 1, 2, 0):
            to = column(j)
            code = info[b, pl.ds(z * plane + to, 1), :]
            pick = jnp.where(code == slot_row, 1.0, 0.0).astype(BF)
            for n in range(width // 256):
                cols = slice(n * 256, (n + 1) * 256)
                value = jnp.dot(pick, blk[b, :, cols], preferred_element_type=F32).astype(BF)
                if j == 0:
                    slots[b, slots_of(c), cols] = value
                else:
                    picked[b, to, :, cols] = value
            if j > 0:
                disp(b, to).start()

    def give(b, to):
        return remote(
            outb.at[b, slots_of(to), :], ret.at[b, c],
            ret_send.at[b, to], ret_recv.at[b, c], {"local": z * plane + to},
        )

    def give_from(b, i):
        return remote(
            outb.at[b, slots_of(i), :], ret.at[b, i],
            ret_send.at[b, i], ret_recv.at[b, i], {"local": z * plane + i},
        )

    def keep(b):
        return pltpu.make_async_copy(outb.at[b, slots_of(c), :], ret.at[b, c], keep_sem.at[b])

    def run(b):
        for j in range(1, plane):
            disp_from(b, column(j)).wait_recv()

        def for_other(n, carry):
            cols = pl.ds(pl.multiple_of(n * 256, 256), 256)
            psend[b, :, cols] = jnp.dot(
                slots[b], w_oth[:, cols], preferred_element_type=F32
            ).astype(BF)
            return carry

        lax.fori_loop(0, 2 * inner // 256, for_other, 0)
        part = remote(psend.at[b], precv.at[b], gu_send.at[b], gu_recv.at[b], {"node": other})
        part.start()

        def for_me(n, carry):
            cols = pl.ds(pl.multiple_of(n * 256, 256), 256)
            mine[:, cols] = jnp.dot(slots[b], w_mine[:, cols], preferred_element_type=F32)
            return carry

        lax.fori_loop(0, 2 * inner // 256, for_me, 0)
        part.wait()

        def act(i, carry):
            r = slots_of(i)
            gate = mine[r, 0:inner] + precv[b, r, 0:inner].astype(F32)
            upv = mine[r, inner:2 * inner] + precv[b, r, inner:2 * inner].astype(F32)
            gate = gate * gate_scale[...]
            hid[b, nd, r, :] = (gate / (1.0 + jnp.exp(-gate)) * (upv * up_scale[...])).astype(BF)
            return carry

        lax.fori_loop(0, plane, act, 0)
        swap = remote(
            hid.at[b, nd], hid.at[b, nd], hid_send.at[b], hid_recv.at[b], {"node": other}
        )
        swap.start()
        swap.wait()

        def project(n, carry):
            cols = pl.ds(pl.multiple_of(n * 256, 256), 256)
            value = jnp.dot(hid[b, 0], wd[0:inner, cols], preferred_element_type=F32)
            value = value + jnp.dot(
                hid[b, 1], wd[inner:2 * inner, cols], preferred_element_type=F32
            )
            outb[b, :, cols] = (value * ds[:, cols]).astype(BF)
            return carry

        lax.fori_loop(0, width // 256, project, 0)
        for j in (3, 1, 2):
            give(b, column(j)).start()
        keep(b).start()

    lane = lax.broadcasted_iota(jnp.int32, (rows, 128), 1)
    slot_lane = lax.broadcasted_iota(jnp.int32, (rows, cap), 1).astype(F32)

    def home(b):
        to = {"local": b * plane + c}
        return (
            remote(part_out.at[b], part_in.at[z], back_send.at[0, b], back_recv.at[0, z], to),
            remote(dots_out.at[b], dots_in.at[z], back_send.at[1, b], back_recv.at[1, z], to),
        )

    def home_from(b):
        to = {"local": b * plane + c}
        return (
            remote(part_out.at[b], part_in.at[b], back_send.at[0, b], back_recv.at[0, b], to),
            remote(dots_out.at[b], dots_in.at[b], back_send.at[1, b], back_recv.at[1, b], to),
        )

    def combine(b, stays):
        acc[...] = jnp.zeros_like(acc)
        dots[...] = jnp.zeros_like(dots)
        table[...] = jnp.concatenate(
            [info[b], jnp.zeros((128 - 2 * experts, rows), F32)], axis=0
        ).T

        def one(j, carry):
            i = column(j)

            @pl.when(j > 0)
            def _():
                give_from(b, i).wait_recv()

            at_e = lane == z * plane + i
            slot = jnp.sum(jnp.where(at_e, table[...], 0.0), axis=1, keepdims=True)
            at_p = lane == experts + z * plane + i
            prob = jnp.sum(jnp.where(at_p, table[...], 0.0), axis=1, keepdims=True)
            pick = jnp.where(slot == slot_lane, 1.0, 0.0).astype(BF)
            total = jnp.zeros((rows, 1), F32)
            for n in range(width // 256):
                cols = slice(n * 256, (n + 1) * 256)
                got = jnp.dot(pick, ret[b, i, :, cols], preferred_element_type=F32)
                acc[:, cols] += got * prob
                total = total + jnp.sum(
                    got * cotb[b, :, cols].astype(F32), axis=1, keepdims=True
                )
            dots[...] = jnp.where(at_e, total, dots[...])
            return carry

        keep(b).wait()
        lax.fori_loop(0, plane, one, 0)
        if stays:
            part_in[b] = acc[...].astype(BF)
            dots_in[b] = dots[...].T[0:experts, :]
        else:
            part_out[b] = acc[...].astype(BF)
            dots_out[b] = dots[...].T[0:experts, :]
            for copy in home(b):
                copy.start()

    spread(0, (0, 1))
    for copy in loads:
        copy.start()
    share = remote(
        w_down.at[0, :, oth_feat], wd.at[my_rows, :], core_send.at[0], core_recv.at[0],
        {"node": other},
    )
    share.start()
    dispatch(order[0])
    spread(1, (0, 1))
    dispatch(order[1])
    spread(2, (0, 1))
    dispatch(order[3])
    for copy in loads:
        copy.wait()
    share.wait()
    spread(3, (0, 1))
    dispatch(order[2])
    spread(0, (2,))
    run(order[1])
    spread(1, (2,))
    run(order[3])
    spread(2, (2,))
    run(order[2])
    spread(3, (2,))
    combine(order[1], False)
    run(order[0])
    combine(order[3], False)
    combine(order[2], False)
    combine(order[0], True)

    for s in range(1, levels):
        for copy in home_from((z + s) % levels):
            copy.wait_recv()
    dots_sum[...] = dots_in[0] + dots_in[1] + dots_in[2] + dots_in[3]
    join = remote(dots_sum, dots_core, core_send.at[1], core_recv.at[1], {"node": other})
    join.start()
    for n in range(width // 256):
        cols = slice(n * 256, (n + 1) * 256)
        total = part_in[0, :, cols].astype(F32)
        for i in range(1, levels):
            total = total + part_in[i, :, cols].astype(F32)
        mixed[:, cols] = total.astype(BF)
    join.wait()
    both = dots_sum[...] + dots_core[...]
    for k in range(top):
        gate_grad[k:k + 1, :] = jnp.sum(
            jnp.where(ids[k:k + 1, :] == expert_row, both, 0.0), axis=0, keepdims=True
        )

    for s in range(levels):
        spread_done(s)
    for i in range(levels):
        for j in range(1, plane):
            disp(i, column(j)).wait_send()
            give(i, column(j)).wait_send()
    for s in range(1, levels):
        for copy in home((z + s) % levels):
            copy.wait_send()


def fused(
    tokens, expert_ids, gate_probs, w_gate, w_up, w_down, gate_scale, up_scale, down_scale, cotangent
):
    experts = lax.axis_size("local")
    rows, top = expert_ids.shape
    cap = max(2, min(rows, rows * top * 5 // (4 * experts)))
    width = tokens.shape[1]
    inner = w_down.shape[1]
    plane = 4
    levels = experts // plane
    m = plane * cap
    vm = pl.BlockSpec(memory_space=pltpu.VMEM)
    hbm = pl.BlockSpec(memory_space=pl.ANY)
    dma = pltpu.SemaphoreType.DMA
    mixed, gate_grad = pl.pallas_call(
        layer_kernel,
        out_shape=(
            jax.ShapeDtypeStruct((rows, width), BF),
            jax.ShapeDtypeStruct((top, rows), F32),
        ),
        in_specs=[hbm, vm, vm, hbm, hbm, hbm, vm, vm, hbm, hbm],
        out_specs=(vm, vm),
        scratch_shapes=[
            pltpu.VMEM((levels, rows, width), BF),
            pltpu.VMEM((levels, rows, width), BF),
            pltpu.VMEM((levels, 2 * experts, rows), F32),
            pltpu.VMEM((width, 2 * inner), BF),
            pltpu.VMEM((width, 2 * inner), BF),
            pltpu.VMEM((2 * inner, width), BF),
            pltpu.VMEM((1, width), F32),
            pltpu.VMEM((levels, plane, cap, width), BF),
            pltpu.VMEM((levels, m, width), BF),
            pltpu.VMEM((levels, m, 2 * inner), BF),
            pltpu.VMEM((levels, m, 2 * inner), BF),
            pltpu.VMEM((m, 2 * inner), F32),
            pltpu.VMEM((levels, 2, m, inner), BF),
            pltpu.VMEM((levels, m, width), BF),
            pltpu.VMEM((levels, plane, cap, width), BF),
            pltpu.VMEM((rows, width), F32),
            pltpu.VMEM((levels, rows, width), BF),
            pltpu.VMEM((levels, rows, width), BF),
            pltpu.VMEM((levels, experts, rows), F32),
            pltpu.VMEM((levels, experts, rows), F32),
            pltpu.VMEM((rows, 128), F32),
            pltpu.VMEM((rows, 128), F32),
            pltpu.VMEM((experts, rows), F32),
            pltpu.VMEM((experts, rows), F32),
            dma((6,)),
            dma((2,)),
            dma((levels,)),
            dma((2, 3, levels)),
            dma((3, levels)),
            dma((levels, plane)),
            dma((levels, plane)),
            dma((levels,)),
            dma((levels,)),
            dma((levels,)),
            dma((levels,)),
            dma((levels, plane)),
            dma((levels, plane)),
            dma((2, levels)),
            dma((2, levels)),
            dma((2,)),
            dma((2,)),
        ],
        compiler_params=pltpu.CompilerParams(
            collective_id=0, has_side_effects=True, vmem_limit_bytes=58 * 1024 * 1024
        ),
    )(
        tokens, expert_ids.T, gate_probs.T, w_gate, w_up, w_down, gate_scale, up_scale, down_scale,
        cotangent,
    )
    return mixed, gate_grad.T


def solution(mesh):
    small = mesh.shape["local"] == 16 and mesh.shape["node"] == 2
    return jax.shard_map(
        fused if small else on_device,
        mesh=mesh,
        in_specs=(
            P(("groups", "local"), "node"),
            P(("groups", "local"), None),
            P(("groups", "local"), None),
            P("local", "node", None),
            P("local", "node", None),
            P("local", "node", None),
            P("local", "node"),
            P("local", "node"),
            P("local", None),
            P(("groups", "local"), "node"),
        ),
        out_specs=(P(("groups", "local"), "node"), P(("groups", "local"), None)),
        check_vma=False,
    )
```
